768 devices in a mesh: mesh: 48 (over y, z_lo, core), event: 16 (over z_hi, x).
Axes of the slice: x: 4, y: 8, z: 12 (z_hi: 4, z_lo: 3; z = z_hi * 3 + z_lo), core: 2. Of those that a mesh axis runs over, the one named last changes fastest.
Arguments:
- forward_now: float32 [16, 3, 124848], P('event', None, 'mesh'), may hold values from -6 to 6
- forward_prev: float32 [16, 3, 124848], P('event', None, 'mesh'), may hold values from -6 to 6
- adjoint_now: float32 [16, 3, 124848], P('event', None, 'mesh'), may hold values from -6 to 6
- adjoint_prev: float32 [16, 3, 124848], P('event', None, 'mesh'), may hold values from -6 to 6
- connectivity: int32 [125, 1536], P(None, 'mesh'), may hold values from 0 to 2600, as said below
- lower_face: int32 [48, 289], P('mesh'), may hold values from 0 to 2600, as said below
- upper_face: int32 [48, 289], P('mesh'), may hold values from 0 to 2600, as said below
- bulk_modulus: float32 [125, 1536], P(None, 'mesh'), may hold values from 0.5 to 2
- shear_modulus: float32 [125, 1536], P(None, 'mesh'), may hold values from 0.3 to 1.2
- step_scale: float32 [124848], P('mesh'), may hold values from 0.0069 to 5.01, as said below
- receiver_points: int32 [6144], P('mesh'), may hold values from 0 to 2600
- adjoint_source: float32 [16, 2, 3, 6144], P('event', None, None, 'mesh'), may hold values from -18 to 18
Outputs:
- forward_next: float32 [16, 3, 124848], P('event', None, 'mesh')
- adjoint_next: float32 [16, 3, 124848], P('event', None, 'mesh')
- kernels: float32 [2, 125, 1536], P(None, None, ('mesh', 'event'))
The draws below stay inside these ranges and needn't reach their ends.
Inputs may be any that keep to these rules, and one draw needn't show every extreme that they name: `connectivity`: each column lists local point numbers of its element's partition; every local point is used. A partition's elements come in 2 layers of 16: the first layer holds every point of the partition's lower_face, the last layer every point of its upper_face, and no other element touches those points. `lower_face`: distinct local point numbers, none in upper_face of the same partition; slot s of partition p's lower_face and slot s of partition p-1's upper_face are one shared point. `upper_face`: distinct local point numbers, none in lower_face of the same partition. `step_scale`: Positive.
All inputs are finite; a program needn't handle non-finite values.
Results may differ from the reference program's by a relative error of at most 0.0001.
Values sent between devices are 32-bit elements; how exact they have to be, the bound alone decides.
No kernel may reach another device: no remote copies, remote signals or barrier semaphores. Data moves between devices by JAX's collectives and lax.ppermute only.
A program may use at most 32 MiB of HBM per device.

```python
import math
import jax
import jax.numpy as jnp
import numpy as np
from jax import lax

GLL = 5
EX = 4
EY = 4
EZ = 2
RECV_DEV = 128
STEPS = 2
E = 32
NP = 2601
FACE = 289
PARTITIONS = 48
EVENTS = 16
ELEMS = 1536
NPTS = 124848
RECV = 6144


def local_numbering(key):
    keys = jax.random.split(key, PARTITIONS)

    def one_partition(single):
        return jax.random.permutation(single, NP)
    return jax.vmap(one_partition)(keys).astype(jnp.int32)


def grid_index():
    node = jnp.arange(GLL * GLL * GLL, dtype=jnp.int32)[:, None]
    elem = jnp.arange(E, dtype=jnp.int32)[None, :]
    width_x = (GLL - 1) * EX + 1
    width_y = (GLL - 1) * EY + 1
    along_x = elem % EX * (GLL - 1) + node % GLL
    along_y = elem // EX % EY * (GLL - 1) + node // GLL % GLL
    along_z = elem // (EX * EY) * (GLL - 1) + node // (GLL * GLL)
    return (along_z * width_y + along_y) * width_x + along_x


def edge_weight(index, count, rim):
    phase = index % 4
    base = jnp.where(phase == 0, 0.2, jnp.where(phase == 2, 32.0 / 45.0, 49.0 / 90.0))
    return jnp.where((index == 0) | (index == count - 1), rim, base).astype(jnp.float32)


def draw_connectivity(key, part):
    numbering = local_numbering(key)
    picked = numbering[:, grid_index()]
    return picked.transpose(1, 0, 2).reshape(GLL * GLL * GLL, PARTITIONS * E).astype(jnp.int32)


def draw_lower_face(key, part):
    numbering = local_numbering(key)
    return numbering[:, :FACE].astype(jnp.int32)


def draw_upper_face(key, part):
    numbering = local_numbering(key)
    return numbering[:, NP - FACE:].astype(jnp.int32)


def draw_step_scale(key, part):
    numbering = local_numbering(key)
    key = jax.random.fold_in(key, 7)
    width_x = (GLL - 1) * EX + 1
    width_y = (GLL - 1) * EY + 1
    width_z = (GLL - 1) * EZ + 1
    position = jnp.arange(NP, dtype=jnp.int32)
    index_x = position % width_x
    index_y = position // width_x % width_y
    index_z = position // (width_x * width_y)
    weight = edge_weight(index_x, width_x, 0.1) * edge_weight(index_y, width_y, 0.1) * edge_weight(index_z, width_z, 0.2)
    spread = jnp.exp(jax.random.uniform(key, (PARTITIONS, NP), jnp.float32, math.log(0.5), math.log(2.0)))
    scale_grid = 0.005 * spread / weight[None, :]
    rows = jnp.arange(PARTITIONS, dtype=jnp.int32)[:, None]
    placed = jnp.zeros((PARTITIONS, NP), jnp.float32).at[rows, numbering].set(scale_grid)
    return placed.reshape(PARTITIONS * NP)


def place_ends(result, key, low, largest):
    dims = result.shape
    place = [jax.random.randint(jax.random.fold_in(key, axis), (), 0, dims[axis]) for axis in range(len(dims))]
    result = result.at[tuple(place)].set(low)
    longest = dims.index(max(dims))
    place[longest] = (place[longest] + 1) % dims[longest]
    return result.at[tuple(place)].set(largest)


def block_levels(key, shape, shards, low, largest):
    gain = 1.0
    for dim, shards_of in shards:
        heights = jax.random.uniform(jax.random.fold_in(jax.random.fold_in(key, 6), dim), (shards_of,), jnp.float32, low / len(shards), largest / len(shards))
        gain = gain * jnp.repeat(jnp.exp(heights), shape[dim] // shards_of).reshape((-1,) + (1,) * (len(shape) - 1 - dim))
    return gain


def centred(key, extent, width, limit, cuts=(), kind=jnp.bfloat16):
    values = width * jax.random.normal(key, extent, jnp.float32)
    if cuts:
        values = values * block_levels(key, extent, cuts, -0.22, 0.18)
    return jnp.clip(values, -limit, limit).astype(kind)


def setup_inputs(seed: int = 0) -> dict:
    arg_keys = jax.random.split(jax.random.key(seed), 13)
    forward_now = centred(arg_keys[0], (EVENTS, 3, NPTS), 1.0, 6.0, ((0, 16), (2, 48)), jnp.float32)
    forward_prev = centred(arg_keys[1], (EVENTS, 3, NPTS), 1.0, 6.0, ((0, 16), (2, 48)), jnp.float32)
    adjoint_now = centred(arg_keys[2], (EVENTS, 3, NPTS), 1.0, 6.0, ((0, 16), (2, 48)), jnp.float32)
    adjoint_prev = centred(arg_keys[3], (EVENTS, 3, NPTS), 1.0, 6.0, ((0, 16), (2, 48)), jnp.float32)
    connectivity = draw_connectivity(jax.random.fold_in(arg_keys[12], 71), 0)
    lower_face = draw_lower_face(jax.random.fold_in(arg_keys[12], 71), 0)
    upper_face = draw_upper_face(jax.random.fold_in(arg_keys[12], 71), 0)
    bulk_modulus = jnp.clip(jnp.exp(math.log(2.0) - 1.3862944 * jax.random.uniform(arg_keys[7], (GLL * GLL * GLL, ELEMS), jnp.float32) ** block_levels(arg_keys[7], (GLL * GLL * GLL, ELEMS), ((1, 48),), -0.2, 0.2)), 0.5, 2.0)
    shear_modulus = jnp.clip(jnp.exp(math.log(1.2) - 1.3862944 * jax.random.uniform(arg_keys[8], (GLL * GLL * GLL, ELEMS), jnp.float32) ** block_levels(arg_keys[8], (GLL * GLL * GLL, ELEMS), ((1, 48),), -0.2, 0.2)), 0.3, 1.2)
    step_scale = draw_step_scale(jax.random.fold_in(arg_keys[12], 71), 0)
    receiver_points = place_ends(jax.random.randint(arg_keys[10], (RECV,), 0, NP), jax.random.fold_in(arg_keys[10], 1), 0, NP - 1).astype(jnp.int32)
    adjoint_source = centred(arg_keys[11], (EVENTS, STEPS, 3, RECV), 3.0, 18.0, ((0, 16), (3, 48)), jnp.float32)
    return {"forward_now": forward_now, "forward_prev": forward_prev, "adjoint_now": adjoint_now, "adjoint_prev": adjoint_prev, "connectivity": connectivity, "lower_face": lower_face, "upper_face": upper_face, "bulk_modulus": bulk_modulus, "shear_modulus": shear_modulus, "step_scale": step_scale, "receiver_points": receiver_points, "adjoint_source": adjoint_source}


kernel_weight = 0.02

def derivative_table():
    root = math.sqrt(3.0 / 7.0)
    points = [-1.0, -root, 0.0, root, 1.0]
    legendre = [(35.0 * x ** 4 - 30.0 * x ** 2 + 3.0) / 8.0 for x in points]
    table = np.zeros((5, 5))
    for row in range(5):
        for column in range(5):
            if row != column:
                table[row, column] = legendre[row] / legendre[column] / (points[row] - points[column])
    table[0, 0] = -2.5
    table[4, 4] = 2.5
    return table

def cube_weights():
    line = np.array([0.1, 49.0 / 90.0, 32.0 / 45.0, 49.0 / 90.0, 0.1])
    cube = line[:, None, None] * line[None, :, None] * line[None, None, :]
    return cube.reshape(125, 1)

def element_terms(values, kappa, shear_mod, deriv, quad):
    count = values.shape[-1]
    top = lax.Precision.HIGHEST
    cube = values.reshape(2, 3, 5, 5, 5, count)
    grad_x = jnp.einsum('ap,fjcbpe->fjcbae', deriv, cube, precision=top)
    grad_y = jnp.einsum('bp,fjcpae->fjcbae', deriv, cube, precision=top)
    grad_z = jnp.einsum('cp,fjpbae->fjcbae', deriv, cube, precision=top)
    grads = jnp.stack([grad_x, grad_y, grad_z]).reshape(3, 2, 3, 125, count).transpose(0, 2, 1, 3, 4)
    strain = 0.5 * (grads + grads.transpose(1, 0, 2, 3, 4))
    dilation = strain[0, 0] + strain[1, 1] + strain[2, 2]
    unit = jnp.eye(3, dtype=jnp.float32)[:, :, None, None, None]
    deviator = strain - unit * (dilation / 3.0)
    stress = unit * (kappa * dilation) + 2.0 * shear_mod * deviator
    bulk = -kernel_weight * kappa * dilation[0] * dilation[1]
    shear = -2.0 * kernel_weight * shear_mod * lax.optimization_barrier(jnp.sum(deviator[:, :, 0] * deviator[:, :, 1], axis=(0, 1)))
    weighted = (quad * stress).reshape(3, 3, 2, 5, 5, 5, count)
    back = jnp.einsum('pa,jfcbpe->jfcbae', deriv, weighted[0], precision=top)
    back = back + jnp.einsum('pb,jfcpae->jfcbae', deriv, weighted[1], precision=top)
    back = back + jnp.einsum('pc,jfpbae->jfcbae', deriv, weighted[2], precision=top)
    forces = -back.transpose(1, 0, 2, 3, 4, 5).reshape(2, 3, 125, count)
    return (forces, bulk, shear)

def reference(forward_now, forward_prev, adjoint_now, adjoint_prev, connectivity, lower_face, upper_face, bulk_modulus, shear_modulus, step_scale, receiver_points, adjoint_source):
    deriv = jnp.asarray(derivative_table(), jnp.float32)
    quad = jnp.asarray(cube_weights(), jnp.float32)
    offsets = jnp.arange(ELEMS, dtype=jnp.int32) // E * NP
    nodes = (connectivity + offsets[None, :]).astype(jnp.int32)
    part_start = (jnp.arange(PARTITIONS, dtype=jnp.int32) * NP)[:, None]
    lower_all = (lower_face + part_start).astype(jnp.int32)
    upper_all = (upper_face + part_start).astype(jnp.int32)
    receivers = (receiver_points + jnp.arange(RECV, dtype=jnp.int32) // RECV_DEV * NP).astype(jnp.int32)

    def one_event(totals, inputs):
        fwd_now, fwd_prev, adj_now, adj_prev, sources = inputs
        waves = jnp.stack([fwd_now, adj_now])
        before = jnp.stack([fwd_prev, adj_prev])
        for step in range(STEPS):
            values = waves[:, :, nodes]
            element_force, bulk, shear = element_terms(values, bulk_modulus, shear_modulus, deriv, quad)
            injected = jnp.zeros((3, NPTS), jnp.float32).at[:, receivers].add(sources[step])
            forces = jnp.stack([jnp.zeros_like(injected), injected])
            forces = forces.at[:, :, nodes].add(element_force)
            upward = forces[:, :, upper_all]
            downward = forces[:, :, lower_all]
            blank = jnp.zeros((2, 3, 1, FACE), jnp.float32)
            below = jnp.concatenate([blank, upward[:, :, :-1]], 2)
            above = jnp.concatenate([downward[:, :, 1:], blank], 2)
            forces = forces.at[:, :, lower_all].add(below).at[:, :, upper_all].add(above)
            following = 2.0 * waves - before + step_scale * forces
            before = waves
            waves = following
            totals = totals + jnp.stack([bulk, shear])
        return (totals, (waves[0], waves[1]))
    start = jnp.zeros((2, 125, ELEMS), jnp.float32)
    totals, results = lax.scan(one_event, start, (forward_now, forward_prev, adjoint_now, adjoint_prev, adjoint_source))
    return (results[0], results[1], totals)
```

```python
import functools
import math

import jax
import jax.numpy as jnp
import numpy as np
from jax import lax
from jax.experimental import pallas as pl
from jax.experimental.pallas import tpu as pltpu
from jax.sharding import PartitionSpec as P

F32 = jnp.float32
BF16 = jnp.bfloat16
EVENTS = 16
FIELDS = 6
ELEMS = 32
CUBE = 125
POINTS = 2601
FACE = 289
LANES = 128
WIDE = 256
FINE = 21
COARSE = 11
PADDED = COARSE * WIDE
RECEIVER_ROW = 32
FACE_ROW = 40
KERNEL_WEIGHT = 0.02

VMEM = pl.BlockSpec(memory_space=pltpu.VMEM)
MIB = 1024 * 1024


def derivative_table():
    root = math.sqrt(3.0 / 7.0)
    points = [-1.0, -root, 0.0, root, 1.0]
    legendre = [(35.0 * x**4 - 30.0 * x**2 + 3.0) / 8.0 for x in points]
    table = np.zeros((5, 5))
    for row in range(5):
        for column in range(5):
            if row != column:
                table[row, column] = (
                    legendre[row] / legendre[column] / (points[row] - points[column])
                )
    table[0, 0] = -2.5
    table[4, 4] = 2.5
    return table


def cube_tables():
    deriv = derivative_table().astype(np.float32).astype(np.float64)
    line = np.array([0.1, 49.0 / 90.0, 32.0 / 45.0, 49.0 / 90.0, 0.1])
    cube = (line[:, None, None] * line[None, :, None] * line[None, None, :]).reshape(CUBE)
    cube = cube.astype(np.float32).astype(np.float64)
    along = [
        np.kron(np.eye(25), deriv),
        np.kron(np.eye(5), np.kron(deriv, np.eye(5))),
        np.kron(deriv, np.eye(25)),
    ]
    ahead = np.zeros((3 * LANES, LANES))
    back = np.zeros((3 * LANES, LANES))
    for i in range(3):
        ahead[i * LANES : i * LANES + CUBE, :CUBE] = along[i]
        back[i * LANES : i * LANES + CUBE, :CUBE] = -cube[:, None] * along[i]
    return (jnp.asarray(ahead, F32), jnp.asarray(back, F32))


def split(value):
    high = value.astype(BF16)
    return (high, (value - high.astype(F32)).astype(BF16))


def product(value, table, side):
    high, low = split(value)
    table_high, table_low = split(table)

    def dot(a, b):
        return lax.dot_general(a, b, (((1,), (side,)), ((), ())), preferred_element_type=F32)

    return dot(high, table_high) + (dot(low, table_high) + dot(high, table_low))


def pick(row, lanes):
    return jnp.take_along_axis(row, lanes, axis=1, mode="promise_in_bounds")


def gather_elements(wave_ref, index):
    fine = index >> 7
    lane = index & 127
    found = [jnp.zeros((ELEMS, LANES), F32) for _ in range(FIELDS)]
    for c in range(FINE):
        hit = fine == c
        for r in range(FIELDS):
            row = wave_ref[r : r + 1, c * LANES : (c + 1) * LANES]
            got = pick(jnp.broadcast_to(row, (ELEMS, LANES)), lane)
            found[r] = jnp.where(hit, got, found[r])
    return found


def gather_faces(forces, index_ref, inner_ref, outer_ref):
    for tile in range(6):
        index = jnp.broadcast_to(index_ref[FACE_ROW + tile : FACE_ROW + tile + 1, :], (8, LANES))
        fine = index >> 7
        lane = index & 127
        found = jnp.zeros((8, LANES), F32)
        for c in range(FINE):
            block = forces[c // 2][:, (c % 2) * LANES : (c % 2 + 1) * LANES]
            found = jnp.where(fine == c, pick(block, lane), found)
        if tile < 3:
            inner_ref[tile * 8 : tile * 8 + 8, :] = found
        else:
            outer_ref[(tile - 3) * 8 : (tile - 3) * 8 + 8, :] = found


def scatter(tiles, rows, index_ref, left_ref, right_ref):
    step = lax.broadcasted_iota(jnp.int32, (16, LANES), 0)
    for t, (tile, row) in enumerate(zip(tiles, rows)):
        lanes = slice(t * LANES, (t + 1) * LANES)
        index = jnp.broadcast_to(index_ref[row : row + 1, :], (16, LANES))
        coarse = (index >> 8).astype(F32).astype(BF16)
        offset = ((index & 255) - step).astype(F32).astype(BF16)
        high = tile.astype(BF16).astype(F32)
        both = jnp.concatenate([high, tile - high], 0).astype(BF16)
        for c in range(COARSE):
            left_ref[c * 16 : (c + 1) * 16, lanes] = jnp.where(coarse == c, both, jnp.zeros_like(both))
        for c in range(16):
            right_ref[c * 16 : (c + 1) * 16, lanes] = jnp.where(
                offset == c * 16, jnp.ones_like(both), jnp.zeros_like(both)
            )
    width = len(rows) * LANES
    total = lax.dot_general(
        left_ref[:, :width],
        right_ref[:, :width],
        (((1,), (1,)), ((), ())),
        preferred_element_type=F32,
    )
    return [total[c * 16 : c * 16 + 8] + total[c * 16 + 8 : c * 16 + 16] for c in range(COARSE)]


def element_terms(fields, kappa, shear_mod, ahead, back):
    grads = product(jnp.concatenate(fields, 0), ahead[...], 1)

    def grad(f, i, j):
        r = (3 * f + j) * ELEMS
        return grads[r : r + ELEMS, i * LANES : (i + 1) * LANES]

    columns = []
    dilations = []
    deviators = []
    for f in range(2):
        normal = [grad(f, i, i) for i in range(3)]
        dilation = normal[0] + normal[1] + normal[2]
        deviator = [n - dilation * (1.0 / 3.0) for n in normal]
        shear = {
            (i, j): 0.5 * (grad(f, i, j) + grad(f, j, i)) for i, j in ((0, 1), (0, 2), (1, 2))
        }
        pressure = kappa * dilation
        twice = 2.0 * shear_mod
        for j in range(3):
            stress = [
                pressure + twice * deviator[j] if i == j else twice * shear[min(i, j), max(i, j)]
                for i in range(3)
            ]
            columns.append(jnp.concatenate(stress, 1))
        dilations.append(dilation)
        deviators.append((deviator, shear))
    bulk = -KERNEL_WEIGHT * kappa * dilations[0] * dilations[1]
    (normal0, shear0), (normal1, shear1) = deviators
    inner = normal0[0] * normal1[0] + normal0[1] * normal1[1] + normal0[2] * normal1[2]
    cross = sum(shear0[key] * shear1[key] for key in shear0)
    shear = -2.0 * KERNEL_WEIGHT * shear_mod * (inner + 2.0 * cross)
    forces = product(jnp.concatenate(columns, 0), back[...], 0)
    return (forces, bulk, shear)


def local_step(wave_ref, moduli_ref, index_ref, source_ref, step, tables, tile_ref, left_ref, right_ref):
    kappa = moduli_ref[0:ELEMS, :]
    shear_mod = moduli_ref[ELEMS : 2 * ELEMS, :]
    fields = gather_elements(wave_ref, index_ref[0:ELEMS, :])
    element_force, bulk, shear = element_terms(fields, kappa, shear_mod, *tables)
    tile_ref[...] = jnp.zeros_like(tile_ref)
    for r in range(FIELDS):
        tile_ref[pl.ds(r, ELEMS, stride=8), :] = element_force[r * ELEMS : (r + 1) * ELEMS]
    for j in range(3):
        row = RECEIVER_ROW * 8 + 3 + j
        tile_ref[row : row + 1, :] = source_ref[j, step : step + 1, :]
    count = RECEIVER_ROW + 2
    tiles = [tile_ref[8 * t : 8 * t + 8, :] for t in range(count)]
    forces = scatter(tiles, list(range(count)), index_ref, left_ref, right_ref)
    return (forces, bulk, shear)


def add_faces(inner_ref, outer_ref, index_ref, left_ref, right_ref):
    tiles = [ref[8 * t : 8 * t + 8, :] for ref in (inner_ref, outer_ref) for t in range(3)]
    return scatter(tiles, [FACE_ROW + t for t in range(6)], index_ref, left_ref, right_ref)


def block(c):
    return slice(c * WIDE, (c + 1) * WIDE)


def first_kernel(*refs):
    inputs, refs = refs[:14], refs[14:]
    wave, force, index, moduli, to_inner, to_outer, totals = refs[:7]
    kept, refs = refs[7:13], refs[13:]
    source, tables = kept[0], kept[4:]
    arrived, (tiles, left, right, sems) = refs[:8], refs[8:]
    copies = [
        pltpu.make_async_copy(source, target, sems.at[i])
        for i, (source, target) in enumerate(zip(inputs, arrived + kept))
    ]
    for copy in copies:
        copy.start()
    forward, adjoint, connectivity, receivers, lower, upper, bulk_modulus, shear_modulus = arrived
    for ref in (wave, moduli):
        ref[...] = jnp.zeros_like(ref)
    index[0:FACE_ROW, :] = jnp.zeros((FACE_ROW, LANES), jnp.int32)
    index[FACE_ROW:, :] = jnp.full((8, LANES), -1, jnp.int32)
    for copy in copies[:9] + copies[12:]:
        copy.wait()
    for j in range(3):
        wave[j : j + 1, 0:POINTS] = forward[j]
        wave[3 + j : 4 + j, 0:POINTS] = adjoint[j]
    index[0:ELEMS, 0:CUBE] = connectivity[...]
    index[RECEIVER_ROW : RECEIVER_ROW + 1, :] = receivers[...]
    even = lax.rem(lax.axis_index("mesh"), 2) == 0
    inner = jnp.where(even, upper[...], lower[...])
    outer = jnp.where(even, lower[...], upper[...])
    for t in range(3):
        size = min(LANES, FACE - t * LANES)
        part = slice(t * LANES, t * LANES + size)
        index[FACE_ROW + t : FACE_ROW + t + 1, 0:size] = inner[:, part]
        index[FACE_ROW + 3 + t : FACE_ROW + 4 + t, 0:size] = outer[:, part]
    moduli[0:ELEMS, 0:CUBE] = bulk_modulus[...]
    moduli[ELEMS : 2 * ELEMS, 0:CUBE] = shear_modulus[...]
    forces, bulk, shear = local_step(wave, moduli, index, source, 0, tables, tiles, left, right)
    gather_faces(forces, index, to_inner, to_outer)
    for c in range(COARSE):
        force[:, block(c)] = forces[c]
    totals[0:ELEMS, :] = bulk
    totals[ELEMS : 2 * ELEMS, :] = shear
    for copy in copies[9:12]:
        copy.wait()


def second_kernel(
    from_inner,
    from_outer,
    wave,
    force,
    forward_prev,
    adjoint_prev,
    step_scale,
    index,
    moduli,
    source,
    earlier,
    ahead,
    back,
    following,
    scale,
    to_inner,
    to_outer,
    terms,
    now,
    sums,
    tiles,
    left,
    right,
):
    scale[...] = jnp.zeros_like(scale)
    following[...] = jnp.zeros_like(following)
    scale[0:1, 0:POINTS] = step_scale[...].reshape(1, POINTS)
    for j in range(3):
        following[j : j + 1, 0:POINTS] = forward_prev[j]
        following[3 + j : 4 + j, 0:POINTS] = adjoint_prev[j]
    added = add_faces(from_inner, from_outer, index, left, right)
    for c in range(COARSE):
        now[:, block(c)] = (
            2.0 * wave[:, block(c)]
            - following[:, block(c)]
            + scale[0:1, block(c)] * (force[:, block(c)] + added[c])
        )
    tables = (ahead, back)
    forces, bulk, shear = local_step(now, moduli, index, source, 1, tables, tiles, left, right)
    gather_faces(forces, index, to_inner, to_outer)
    for c in range(COARSE):
        following[:, block(c)] = (
            2.0 * now[:, block(c)] - wave[:, block(c)] + scale[0:1, block(c)] * forces[c]
        )
    sums[0:ELEMS, :] = earlier[0:ELEMS, :] + bulk
    sums[ELEMS : 2 * ELEMS, :] = earlier[ELEMS : 2 * ELEMS, :] + shear
    for which in range(2):
        for e in range(2):
            terms[:, 2 * which + e, :] = sums[pl.ds(which * ELEMS + e, EVENTS, stride=2), :]


def third_kernel(from_inner, from_outer, local, scale, index, terms, forward, adjoint, kernels, now, left, right):
    added = add_faces(from_inner, from_outer, index, left, right)
    for c in range(COARSE):
        now[:, block(c)] = local[:, block(c)] + scale[0:1, block(c)] * added[c]
    for j in range(3):
        forward[j] = now[j : j + 1, 0:POINTS]
        adjoint[j] = now[3 + j : 4 + j, 0:POINTS]
    owned = jnp.sum(terms[...], axis=0)
    for which in range(2):
        kernels[which] = owned[2 * which : 2 * which + 2, 0:CUBE]


def call(kernel, outs, scratch, args, place=VMEM):
    return pl.pallas_call(
        kernel,
        out_shape=[jax.ShapeDtypeStruct(shape, dtype) for shape, dtype in outs],
        in_specs=[place] * len(args),
        out_specs=[VMEM] * len(outs),
        scratch_shapes=scratch,
        compiler_params=pltpu.CompilerParams(vmem_limit_bytes=16 * MIB),
    )(*args)


def swap_faces(to_inner, to_outer):
    count = lax.axis_size("mesh")
    inner = [(i, i ^ 1) for i in range(count)]
    outer = [(i, i + 1 if i % 2 else i - 1) for i in range(1, count - 1)]
    return (lax.ppermute(to_inner, "mesh", inner), lax.ppermute(to_outer, "mesh", outer))


def shards(
    forward_now,
    forward_prev,
    adjoint_now,
    adjoint_prev,
    connectivity,
    lower_face,
    upper_face,
    bulk_modulus,
    shear_modulus,
    step_scale,
    receiver_points,
    adjoint_source,
):
    def rows(field):
        return field.transpose(1, 0, 2)

    tables = cube_tables()
    source = adjoint_source[0].transpose(1, 0, 2)
    padded = ((8, PADDED), F32)
    face = ((24, LANES), F32)
    pair = ((2 * ELEMS, LANES), F32)
    wide = (RECEIVER_ROW + 2) * LANES
    work = [
        pltpu.VMEM(((RECEIVER_ROW + 2) * 8, LANES), F32),
        pltpu.VMEM((COARSE * 16, wide), BF16),
        pltpu.VMEM((WIDE, wide), BF16),
    ]
    inputs = [
        rows(forward_now),
        rows(adjoint_now),
        connectivity.T,
        receiver_points.reshape(1, LANES),
        lower_face,
        upper_face,
        bulk_modulus.T,
        shear_modulus.T,
        source,
        rows(forward_prev),
        rows(adjoint_prev),
        step_scale,
        *tables,
    ]
    inputs = [pltpu.with_memory_space_constraint(value, pltpu.HBM) for value in inputs]
    wave, force, index, moduli, to_inner, to_outer, earlier, *kept = call(
        first_kernel,
        [padded, padded, ((48, LANES), jnp.int32), pair, face, face, pair]
        + [(value.shape, value.dtype) for value in inputs[8:]],
        [pltpu.VMEM(value.shape, value.dtype) for value in inputs[:8]]
        + work
        + [pltpu.SemaphoreType.DMA((len(inputs),))],
        inputs,
        pl.BlockSpec(memory_space=pl.ANY),
    )
    from_inner, from_outer = swap_faces(to_inner, to_outer)
    local, scale, to_inner, to_outer, terms = call(
        second_kernel,
        [padded, ((1, PADDED), F32), face, face, ((EVENTS, 4, LANES), F32)],
        [pltpu.VMEM(*padded), pltpu.VMEM(*pair)] + work,
        [
            from_inner,
            from_outer,
            wave,
            force,
            *kept[1:4],
            index,
            moduli,
            kept[0],
            earlier,
            *kept[4:],
        ],
    )
    from_inner, from_outer = swap_faces(to_inner, to_outer)
    terms = lax.all_to_all(terms, "event", 0, 0, tiled=True)
    forward, adjoint, kernels = call(
        third_kernel,
        [((3, 1, POINTS), F32), ((3, 1, POINTS), F32), ((2, 2, CUBE), F32)],
        [
            pltpu.VMEM(*padded),
            pltpu.VMEM((COARSE * 16, 6 * LANES), BF16),
            pltpu.VMEM((WIDE, 6 * LANES), BF16),
        ],
        [from_inner, from_outer, local, scale, index, terms],
    )
    return (rows(forward), rows(adjoint), kernels.transpose(0, 2, 1))


def solution(mesh):
    placed = (
        P("event", None, "mesh"),
        P("event", None, "mesh"),
        P("event", None, "mesh"),
        P("event", None, "mesh"),
        P(None, "mesh"),
        P("mesh", None),
        P("mesh", None),
        P(None, "mesh"),
        P(None, "mesh"),
        P("mesh"),
        P("mesh"),
        P("event", None, None, "mesh"),
    )
    return jax.shard_map(
        shards,
        mesh=mesh,
        in_specs=placed,
        out_specs=(
            P("event", None, "mesh"),
            P("event", None, "mesh"),
            P(None, None, ("mesh", "event")),
        ),
        check_vma=False,
    )
```

```python
import functools
import math

import jax
import jax.numpy as jnp
import numpy as np
from jax import lax
from jax.experimental import pallas as pl
from jax.experimental.pallas import tpu as pltpu
from jax.sharding import PartitionSpec as P

F32 = jnp.float32
BF16 = jnp.bfloat16
EVENTS = 16
FIELDS = 6
ELEMS = 32
CUBE = 125
POINTS = 2601
FACE = 289
LANES = 128
WIDE = 256
FINE = 21
COARSE = 11
PADDED = COARSE * WIDE
HALF = 16
RECEIVER_ROW = 32
FACE_ROW = 40
SLOT_ROW = 6
FACES = 24
PARITY_ROW = 46
KERNEL_WEIGHT = 0.02

VMEM = pl.BlockSpec(memory_space=pltpu.VMEM)
MIB = 1024 * 1024


def derivative_table():
    root = math.sqrt(3.0 / 7.0)
    points = [-1.0, -root, 0.0, root, 1.0]
    legendre = [(35.0 * x**4 - 30.0 * x**2 + 3.0) / 8.0 for x in points]
    table = np.zeros((5, 5))
    for row in range(5):
        for column in range(5):
            if row != column:
                table[row, column] = (
                    legendre[row] / legendre[column] / (points[row] - points[column])
                )
    table[0, 0] = -2.5
    table[4, 4] = 2.5
    return table


def cube_tables():
    deriv = derivative_table().astype(np.float32).astype(np.float64)
    line = np.array([0.1, 49.0 / 90.0, 32.0 / 45.0, 49.0 / 90.0, 0.1])
    cube = (line[:, None, None] * line[None, :, None] * line[None, None, :]).reshape(CUBE)
    cube = cube.astype(np.float32).astype(np.float64)
    along = [
        np.kron(np.eye(25), deriv),
        np.kron(np.eye(5), np.kron(deriv, np.eye(5))),
        np.kron(deriv, np.eye(25)),
    ]
    ahead = np.zeros((3 * LANES, LANES))
    back = np.zeros((3 * LANES, LANES))
    for i in range(3):
        ahead[i * LANES : i * LANES + CUBE, :CUBE] = along[i]
        back[i * LANES : i * LANES + CUBE, :CUBE] = -cube[:, None] * along[i]
    return (jnp.asarray(ahead, F32), jnp.asarray(back, F32))


def split(value):
    high = value.astype(BF16)
    return (high, (value - high.astype(F32)).astype(BF16))


def product(value, table, side):
    high, low = split(value)
    table_high, table_low = split(table)

    def dot(a, b):
        return lax.dot_general(a, b, (((1,), (side,)), ((), ())), preferred_element_type=F32)

    return dot(high, table_high) + (dot(low, table_high) + dot(high, table_low))


def pick(row, lanes):
    return jnp.take_along_axis(row, lanes, axis=1, mode="promise_in_bounds")


def gather_elements(wave_ref, index_ref, count):
    groups = []
    for t in range(0, ELEMS, 8):
        index = index_ref[t : t + 8, :]
        fine = index >> 7
        lane = index & 127
        found = [jnp.zeros((8, LANES), F32) for _ in range(count)]
        for c in range(FINE):
            hit = fine == c
            for r in range(count):
                row = wave_ref[r : r + 1, c * LANES : (c + 1) * LANES]
                found[r] = jnp.where(hit, pick(jnp.broadcast_to(row, (8, LANES)), lane), found[r])
        groups.append(found)
    return [jnp.concatenate(parts, 0) for parts in zip(*groups)]


def gather_faces(blocks, index_ref, targets):
    for face in range(2):
        for tile in range(3):
            at = FACE_ROW + 3 * face + tile
            index = jnp.broadcast_to(index_ref[at : at + 1, :], (8, LANES))
            fine = index >> 7
            lane = index & 127
            found = jnp.zeros((8, LANES), F32)
            for c in range(FINE):
                part = slice((c % 2) * LANES, (c % 2 + 1) * LANES)
                found = jnp.where(fine == c, pick(blocks[c // 2][:, part], lane), found)
            targets[face][8 * tile : 8 * tile + 8, :] = found


def scatter(tiles, rows, left_ref, right_ref):
    step = lax.broadcasted_iota(jnp.int32, (16, LANES), 0)
    for t, (tile, row) in enumerate(zip(tiles, rows)):
        lanes = slice(t * LANES, (t + 1) * LANES)
        index = jnp.broadcast_to(row, (16, LANES))
        coarse = (index >> 8).astype(F32).astype(BF16)
        offset = ((index & 255) - step).astype(F32).astype(BF16)
        high = tile.astype(BF16).astype(F32)
        both = jnp.concatenate([high, tile - high], 0).astype(BF16)
        for c in range(COARSE):
            left_ref[c * 16 : (c + 1) * 16, lanes] = jnp.where(coarse == c, both, jnp.zeros_like(both))
        for c in range(16):
            right_ref[c * 16 : (c + 1) * 16, lanes] = jnp.where(
                offset == c * 16, jnp.ones_like(both), jnp.zeros_like(both)
            )
    width = len(rows) * LANES
    total = lax.dot_general(
        left_ref[:, :width],
        right_ref[:, :width],
        (((1,), (1,)), ((), ())),
        preferred_element_type=F32,
    )
    return [total[c * 16 : c * 16 + 8] + total[c * 16 + 8 : c * 16 + 16] for c in range(COARSE)]


def strains(fields, ahead):
    count = fields[0].shape[0]
    grads = product(jnp.concatenate(fields, 0), ahead, 1)

    def grad(f, i, j):
        r = (3 * f + j) * count
        return grads[r : r + count, i * LANES : (i + 1) * LANES]

    result = []
    for f in range(2):
        normal = [grad(f, i, i) for i in range(3)]
        dilation = normal[0] + normal[1] + normal[2]
        deviator = [n - dilation * (1.0 / 3.0) for n in normal]
        shear = {
            (i, j): 0.5 * (grad(f, i, j) + grad(f, j, i)) for i, j in ((0, 1), (0, 2), (1, 2))
        }
        result.append((dilation, deviator, shear))
    return result


def kernel_terms(strained, kappa, shear_mod):
    (dilation0, normal0, shear0), (dilation1, normal1, shear1) = strained
    bulk = -KERNEL_WEIGHT * kappa * dilation0 * dilation1
    inner = normal0[0] * normal1[0] + normal0[1] * normal1[1] + normal0[2] * normal1[2]
    cross = sum(shear0[key] * shear1[key] for key in shear0)
    return (bulk, -2.0 * KERNEL_WEIGHT * shear_mod * (inner + 2.0 * cross))


def element_forces(strained, kappa, shear_mod, back):
    twice = 2.0 * shear_mod
    columns = []
    for dilation, deviator, shear in strained:
        pressure = kappa * dilation
        for j in range(3):
            stress = [
                pressure + twice * deviator[j] if i == j else twice * shear[min(i, j), max(i, j)]
                for i in range(3)
            ]
            columns.append(jnp.concatenate(stress, 1))
    return product(jnp.concatenate(columns, 0), back, 0)


def element_tiles(tile_ref, forces, source_ref, step):
    count = forces.shape[0] // FIELDS
    tile_ref[...] = jnp.zeros_like(tile_ref)
    for r in range(FIELDS):
        tile_ref[pl.ds(r, count, stride=8), :] = forces[r * count : (r + 1) * count]
    for j in range(3):
        row = count * 8 + 3 + j
        tile_ref[row : row + 1, :] = source_ref[j, step : step + 1, :]
    return [tile_ref[8 * t : 8 * t + 8, :] for t in range(count + 1)]


def block(c):
    return slice(c * WIDE, (c + 1) * WIDE)


def even_partition():
    return lax.rem(lax.axis_index("mesh"), 2) == 0


def halves_in_order(value, even):
    first, second = value[:HALF], value[HALF:]
    return [jnp.where(even, second, first), jnp.where(even, first, second)]


def first_kernel(*refs):
    inputs, refs = refs[:14], refs[14:]
    wave, force, index, moduli, to_inner, to_outer, totals = refs[:7]
    forward_prev, adjoint_prev, step_scale, source, ahead, back = kept = refs[7:13]
    arrived = refs[13:21]
    tiles, left, right, sems = refs[21:]
    copies = [
        pltpu.make_async_copy(value, target, sems.at[i])
        for i, (value, target) in enumerate(zip(inputs, arrived + kept))
    ]
    for i in (2, 0, 1, 6, 7, 12, 13, 4, 5, 3, 11, 8, 9, 10):
        copies[i].start()
    forward, adjoint, connectivity, receivers, lower, upper, bulk_modulus, shear_modulus = arrived
    for ref in (wave, moduli):
        ref[...] = jnp.zeros_like(ref)
    index[0:FACE_ROW, :] = jnp.zeros((FACE_ROW, LANES), jnp.int32)
    index[FACE_ROW:, :] = jnp.full((8, LANES), -1, jnp.int32)
    for copy in copies[:8]:
        copy.wait()
    for j in range(3):
        wave[j : j + 1, 0:POINTS] = forward[j]
        wave[3 + j : 4 + j, 0:POINTS] = adjoint[j]
    even = even_partition()
    for face, (part, kappa, shear_mod) in enumerate(
        zip(*(halves_in_order(ref[...], even) for ref in (connectivity, bulk_modulus, shear_modulus)))
    ):
        start = face * HALF
        index[start : start + HALF, 0:CUBE] = part
        moduli[start : start + HALF, 0:CUBE] = kappa
        moduli[ELEMS + start : ELEMS + start + HALF, 0:CUBE] = shear_mod
    index[RECEIVER_ROW : RECEIVER_ROW + 1, :] = receivers[...]
    index[PARITY_ROW : PARITY_ROW + 1, :] = jnp.where(even, jnp.ones((1, LANES), jnp.int32), 0)
    faces = (jnp.where(even, upper[...], lower[...]), jnp.where(even, lower[...], upper[...]))
    for t in range(3):
        size = min(LANES, FACE - t * LANES)
        for face in range(2):
            at = FACE_ROW + 3 * face + t
            index[at : at + 1, 0:size] = faces[face][:, t * LANES : t * LANES + size]
    kappa = moduli[0:ELEMS, :]
    shear_mod = moduli[ELEMS : 2 * ELEMS, :]
    fields = gather_elements(wave, index, FIELDS)
    for copy in copies[11:]:
        copy.wait()
    strained = strains(fields, ahead[...])
    bulk, shear = kernel_terms(strained, kappa, shear_mod)
    totals[0:ELEMS, :] = bulk
    totals[ELEMS : 2 * ELEMS, :] = shear
    values = element_tiles(tiles, element_forces(strained, kappa, shear_mod, back[...]), source, 0)
    forces = scatter(values, [index[t : t + 1, :] for t in range(RECEIVER_ROW + 1)], left, right)
    gather_faces(forces, index, (to_inner, to_outer))
    for c in range(COARSE):
        force[:, block(c)] = forces[c]
    for copy in copies[8:11]:
        copy.wait()


def between_kernel(
    wave, force, forward_prev, adjoint_prev, step_scale, index, local, scale, fields, slots, at_inner, at_outer, left, right
):
    scale[...] = jnp.zeros_like(scale)
    local[...] = jnp.zeros_like(local)
    scale[0:1, 0:POINTS] = step_scale[...].reshape(1, POINTS)
    for j in range(3):
        local[j : j + 1, 0:POINTS] = forward_prev[j]
        local[3 + j : 4 + j, 0:POINTS] = adjoint_prev[j]
    row = lax.broadcasted_iota(jnp.int32, (8, LANES), 0)
    lane = lax.broadcasted_iota(jnp.int32, (8, LANES), 1)
    marks = [jnp.where(row == SLOT_ROW, lane + (t * LANES + 1), 0).astype(F32) for t in range(3)]
    rows = [index[FACE_ROW + t : FACE_ROW + t + 1, :] for t in range(6)]
    marked = scatter(marks + marks, rows, left, right)
    wide_row = lax.broadcasted_iota(jnp.int32, (8, WIDE), 0)
    spread = []
    for c in range(COARSE):
        spread.append(jnp.broadcast_to(scale[0:1, block(c)], (8, WIDE)))
        local[:, block(c)] = jnp.where(
            wide_row == SLOT_ROW,
            marked[c],
            2.0 * wave[:, block(c)] - local[:, block(c)] + spread[c] * force[:, block(c)],
        )
    gather_faces(spread, index, (at_inner, at_outer))
    found = gather_elements(local, index, FIELDS + 1)
    for r in range(FIELDS):
        fields[r * ELEMS : (r + 1) * ELEMS, :] = found[r]
    slots[...] = found[SLOT_ROW].astype(jnp.int32) - 1


def second_kernel(
    from_inner, scaled_outer, fields, slots, factors, moduli, earlier, ahead, index, terms, now, sums
):
    added = []
    for face, value in enumerate((factors[...] * from_inner[...], scaled_outer[...])):
        scaled = [value[8 * t : 8 * t + 8, :] for t in range(3)]
        fine = slots[face * HALF : (face + 1) * HALF, :] >> 7
        lane = slots[face * HALF : (face + 1) * HALF, :] & 127
        values = []
        for r in range(FIELDS):
            start = r * ELEMS + face * HALF
            value = fields[start : start + HALF, :]
            for t in range(3):
                got = pick(jnp.broadcast_to(scaled[t][r : r + 1, :], (HALF, LANES)), lane)
                value = value + jnp.where(fine == t, got, 0.0)
            values.append(value)
        added.append(values)
    values = [jnp.concatenate(pair, 0) for pair in zip(*added)]
    for r in range(FIELDS):
        now[r * ELEMS : (r + 1) * ELEMS, :] = values[r]
    found = kernel_terms(strains(values, ahead[...]), moduli[0:ELEMS, :], moduli[ELEMS : 2 * ELEMS, :])
    even = jnp.broadcast_to(index[PARITY_ROW : PARITY_ROW + 1, :], (HALF, LANES)) == 1
    for which in range(2):
        start = which * ELEMS
        total = earlier[start : start + ELEMS, :] + found[which]
        sums[start : start + ELEMS, :] = jnp.concatenate(halves_in_order(total, even), 0)
    for which in range(2):
        for e in range(2):
            terms[:, 2 * which + e, :] = sums[pl.ds(which * ELEMS + e, EVENTS, stride=2), :]


def third_kernel(
    now, moduli, index, source, ahead, back, wave, local, scale, following, to_inner, to_outer, tiles, left, right
):
    strained = strains([now[r * ELEMS : (r + 1) * ELEMS, :] for r in range(FIELDS)], ahead[...])
    forces = element_forces(strained, moduli[0:ELEMS, :], moduli[ELEMS : 2 * ELEMS, :], back[...])
    values = element_tiles(tiles, forces, source, 1)
    forces = scatter(values, [index[t : t + 1, :] for t in range(RECEIVER_ROW + 1)], left, right)
    gather_faces(forces, index, (to_inner, to_outer))
    for c in range(COARSE):
        following[:, block(c)] = (
            2.0 * local[:, block(c)] - wave[:, block(c)] + scale[0:1, block(c)] * forces[c]
        )


def fourth_kernel(
    first_inner, from_inner, first_outer, from_outer, following, scale, index, forward, adjoint, result, left, right
):
    inner = 2.0 * first_inner[...] + from_inner[...]
    outer = 2.0 * first_outer[...] + from_outer[...]
    values = [value[8 * t : 8 * t + 8, :] for value in (inner, outer) for t in range(3)]
    added = scatter(values, [index[FACE_ROW + t : FACE_ROW + t + 1, :] for t in range(6)], left, right)
    for c in range(COARSE):
        result[:, block(c)] = following[:, block(c)] + scale[0:1, block(c)] * added[c]
    for j in range(3):
        forward[j] = result[j : j + 1, 0:POINTS]
        adjoint[j] = result[3 + j : 4 + j, 0:POINTS]


def call(kernel, outs, scratch, args, place=VMEM):
    return pl.pallas_call(
        kernel,
        out_shape=[jax.ShapeDtypeStruct(shape, dtype) for shape, dtype in outs],
        in_specs=[place] * len(args),
        out_specs=[VMEM] * len(outs),
        scratch_shapes=scratch,
        compiler_params=pltpu.CompilerParams(vmem_limit_bytes=24 * MIB),
    )(*args)


def swap_faces(to_inner, to_outer):
    count = lax.axis_size("mesh")
    inner = [(i, i ^ 1) for i in range(count)]
    outer = [(i, i + 1 if i % 2 else i - 1) for i in range(1, count - 1)]
    from_outer = lax.ppermute(to_outer, "mesh", outer)
    return (lax.ppermute(to_inner, "mesh", inner), from_outer)


def scatter_work(tiles):
    return [
        pltpu.VMEM((COARSE * 16, tiles * LANES), BF16),
        pltpu.VMEM((WIDE, tiles * LANES), BF16),
    ]


def shards(
    forward_now,
    forward_prev,
    adjoint_now,
    adjoint_prev,
    connectivity,
    lower_face,
    upper_face,
    bulk_modulus,
    shear_modulus,
    step_scale,
    receiver_points,
    adjoint_source,
):
    def rows(field):
        return field.transpose(1, 0, 2)

    padded = ((8, PADDED), F32)
    face = ((FACES, LANES), F32)
    pair = ((2 * ELEMS, LANES), F32)
    at_elements = ((FIELDS * ELEMS, LANES), F32)
    tiles = pltpu.VMEM(((ELEMS + 1) * 8, LANES), F32)
    inputs = [
        rows(forward_now),
        rows(adjoint_now),
        connectivity.T,
        receiver_points.reshape(1, LANES),
        lower_face,
        upper_face,
        bulk_modulus.T,
        shear_modulus.T,
        rows(forward_prev),
        rows(adjoint_prev),
        step_scale,
        adjoint_source[0].transpose(1, 0, 2),
        *cube_tables(),
    ]
    inputs = [pltpu.with_memory_space_constraint(value, pltpu.HBM) for value in inputs]
    wave, force, index, moduli, to_inner, to_outer, earlier, *kept = call(
        first_kernel,
        [padded, padded, ((48, LANES), jnp.int32), pair, face, face, pair]
        + [(value.shape, value.dtype) for value in inputs[8:]],
        [pltpu.VMEM(value.shape, value.dtype) for value in inputs[:8]]
        + [tiles]
        + scatter_work(ELEMS + 1)
        + [pltpu.SemaphoreType.DMA((len(inputs),))],
        inputs,
        pl.BlockSpec(memory_space=pl.ANY),
    )
    forward_prev, adjoint_prev, step_scale, source, ahead, back = kept
    first_inner, first_outer = swap_faces(to_inner, to_outer)
    local, scale, fields, slots, at_inner, at_outer = call(
        between_kernel,
        [padded, ((1, PADDED), F32), at_elements, ((ELEMS, LANES), jnp.int32), face, face],
        scatter_work(6),
        [wave, force, forward_prev, adjoint_prev, step_scale, index],
    )
    terms, now = call(
        second_kernel,
        [((EVENTS, 4, LANES), F32), at_elements],
        [pltpu.VMEM(*pair)],
        [first_inner, at_outer * first_outer, fields, slots, at_inner, moduli, earlier, ahead, index],
    )
    terms = lax.all_to_all(terms, "event", 0, 0, tiled=True)
    following, to_inner, to_outer = call(
        third_kernel,
        [padded, face, face],
        [tiles] + scatter_work(ELEMS + 1),
        [now, moduli, index, source, ahead, back, wave, local, scale],
    )
    from_inner, from_outer = swap_faces(to_inner, to_outer)
    forward, adjoint = call(
        fourth_kernel,
        [((3, 1, POINTS), F32), ((3, 1, POINTS), F32)],
        [pltpu.VMEM(*padded)] + scatter_work(6),
        [first_inner, from_inner, first_outer, from_outer, following, scale, index],
    )
    kernels = jnp.sum(terms, axis=0)[:, :CUBE].reshape(2, 2, CUBE)
    return (rows(forward), rows(adjoint), kernels.transpose(0, 2, 1))


def solution(mesh):
    placed = (
        P("event", None, "mesh"),
        P("event", None, "mesh"),
        P("event", None, "mesh"),
        P("event", None, "mesh"),
        P(None, "mesh"),
        P("mesh", None),
        P("mesh", None),
        P(None, "mesh"),
        P(None, "mesh"),
        P("mesh"),
        P("mesh"),
        P("event", None, None, "mesh"),
    )
    return jax.shard_map(
        shards,
        mesh=mesh,
        in_specs=placed,
        out_specs=(
            P("event", None, "mesh"),
            P("event", None, "mesh"),
            P(None, None, ("mesh", "event")),
        ),
        check_vma=False,
    )
```

```python
import functools
import math

import jax
import jax.numpy as jnp
import numpy as np
from jax import lax
from jax.experimental import pallas as pl
from jax.experimental.pallas import tpu as pltpu
from jax.sharding import PartitionSpec as P

F32 = jnp.float32
BF16 = jnp.bfloat16
EVENTS = 16
FIELDS = 6
ELEMS = 32
CUBE = 125
POINTS = 2601
FACE = 289
LANES = 128
WIDE = 256
FINE = 21
COARSE = 11
PADDED = COARSE * WIDE
HALF = 16
RECEIVER_ROW = 32
FACE_ROW = 40
PARITY_ROW = 46
SLOT_ROW = 6
SCALE_ROW = 7
OUTER = 512
ORDER = [8, 9, 10, 11, 12, 13, 14, 15, 0, 1, 2, 3, 4, 5, 6, 7]
SENT_KAPPA = FIELDS * HALF
SENT_SHEAR = SENT_KAPPA + HALF
SENT_SLOTS = SENT_SHEAR + HALF
SENT_FACE = SENT_SLOTS + HALF
SENT_SOURCE = SENT_FACE + 24
SENT = SENT_SOURCE + 8
CHUNK = 8
KERNEL_WEIGHT = 0.02

VMEM = pl.BlockSpec(memory_space=pltpu.VMEM)
MIB = 1024 * 1024


def derivative_table():
    root = math.sqrt(3.0 / 7.0)
    points = [-1.0, -root, 0.0, root, 1.0]
    legendre = [(35.0 * x**4 - 30.0 * x**2 + 3.0) / 8.0 for x in points]
    table = np.zeros((5, 5))
    for row in range(5):
        for column in range(5):
            if row != column:
                table[row, column] = (
                    legendre[row] / legendre[column] / (points[row] - points[column])
                )
    table[0, 0] = -2.5
    table[4, 4] = 2.5
    return table


def cube_tables():
    deriv = derivative_table().astype(np.float32).astype(np.float64)
    line = np.array([0.1, 49.0 / 90.0, 32.0 / 45.0, 49.0 / 90.0, 0.1])
    cube = (line[:, None, None] * line[None, :, None] * line[None, None, :]).reshape(CUBE)
    cube = cube.astype(np.float32).astype(np.float64)
    along = [
        np.kron(np.eye(25), deriv),
        np.kron(np.eye(5), np.kron(deriv, np.eye(5))),
        np.kron(deriv, np.eye(25)),
    ]
    ahead = np.zeros((3 * LANES, LANES))
    back = np.zeros((3 * LANES, LANES))
    for i in range(3):
        ahead[i * LANES : i * LANES + CUBE, :CUBE] = along[i]
        back[i * LANES : i * LANES + CUBE, :CUBE] = -cube[:, None] * along[i]
    return (jnp.asarray(ahead, F32), jnp.asarray(back, F32))


def split(value):
    high = value.astype(BF16)
    return (high, (value - high.astype(F32)).astype(BF16))


def product(value, table, side):
    high, low = split(value)
    table_high, table_low = split(table)

    def dot(a, b):
        return lax.dot_general(a, b, (((1,), (side,)), ((), ())), preferred_element_type=F32)

    return dot(high, table_high) + (dot(low, table_high) + dot(high, table_low))


def pick(row, lanes):
    return jnp.take_along_axis(row, lanes, axis=1, mode="promise_in_bounds")


def gather_elements(wave_ref, index_ref, count):
    groups = []
    for t in range(0, ELEMS, 8):
        index = index_ref[t : t + 8, :]
        fine = index >> 7
        lane = index & 127
        found = [jnp.zeros((8, LANES), F32) for _ in range(count)]
        for c in range(FINE):
            hit = fine == c
            for r in range(count):
                row = wave_ref[r : r + 1, c * LANES : (c + 1) * LANES]
                found[r] = jnp.where(hit, pick(jnp.broadcast_to(row, (8, LANES)), lane), found[r])
        groups.append(found)
    return [jnp.concatenate(parts, 0) for parts in zip(*groups)]


def gather_faces(blocks, index_ref, targets):
    for face in range(2):
        for tile in range(3):
            at = FACE_ROW + 3 * face + tile
            index = jnp.broadcast_to(index_ref[at : at + 1, :], (8, LANES))
            fine = index >> 7
            lane = index & 127
            found = jnp.zeros((8, LANES), F32)
            for c in range(FINE):
                part = slice((c % 2) * LANES, (c % 2 + 1) * LANES)
                found = jnp.where(fine == c, pick(blocks[c // 2][:, part], lane), found)
            targets[face][SENT_FACE + 8 * tile : SENT_FACE + 8 * tile + 8, :] = found


def scatter(tiles, rows):
    step = lax.broadcasted_iota(jnp.int32, (16, LANES), 0)
    total = None
    for start in range(0, len(tiles), CHUNK):
        left = []
        right = []
        for tile, row in zip(tiles[start : start + CHUNK], rows[start : start + CHUNK]):
            index = jnp.broadcast_to(row, (16, LANES))
            coarse = (index >> 8).astype(F32).astype(BF16)
            offset = ((index & 255) - step).astype(F32).astype(BF16)
            high = tile.astype(BF16).astype(F32)
            pair = jnp.concatenate([high, tile - high], 0).astype(BF16)
            none = jnp.zeros_like(pair)
            one = jnp.ones_like(pair)
            left.append(jnp.concatenate([jnp.where(coarse == c, pair, none) for c in range(COARSE)], 0))
            right.append(jnp.concatenate([jnp.where(offset == c * 16, one, none) for c in range(16)], 0))
        part = lax.dot_general(
            jnp.concatenate(left, 1),
            jnp.concatenate(right, 1),
            (((1,), (1,)), ((), ())),
            preferred_element_type=F32,
        )
        total = part if total is None else total + part
    return [total[c * 16 : c * 16 + 8] + total[c * 16 + 8 : c * 16 + 16] for c in range(COARSE)]


def strains(fields, ahead):
    count = fields[0].shape[0]
    grads = product(jnp.concatenate(fields, 0), ahead, 1)

    def grad(f, i, j):
        r = (3 * f + j) * count
        return grads[r : r + count, i * LANES : (i + 1) * LANES]

    result = []
    for f in range(2):
        normal = [grad(f, i, i) for i in range(3)]
        dilation = normal[0] + normal[1] + normal[2]
        deviator = [n - dilation * (1.0 / 3.0) for n in normal]
        shear = {
            (i, j): 0.5 * (grad(f, i, j) + grad(f, j, i)) for i, j in ((0, 1), (0, 2), (1, 2))
        }
        result.append((dilation, deviator, shear))
    return result


def kernel_terms(strained, kappa, shear_mod):
    (dilation0, normal0, shear0), (dilation1, normal1, shear1) = strained
    bulk = -KERNEL_WEIGHT * kappa * dilation0 * dilation1
    inner = normal0[0] * normal1[0] + normal0[1] * normal1[1] + normal0[2] * normal1[2]
    cross = sum(shear0[key] * shear1[key] for key in shear0)
    return (bulk, -2.0 * KERNEL_WEIGHT * shear_mod * (inner + 2.0 * cross))


def element_forces(strained, kappa, shear_mod, back):
    twice = 2.0 * shear_mod
    columns = []
    for dilation, deviator, shear in strained:
        pressure = kappa * dilation
        for j in range(3):
            stress = [
                pressure + twice * deviator[j] if i == j else twice * shear[min(i, j), max(i, j)]
                for i in range(3)
            ]
            columns.append(jnp.concatenate(stress, 1))
    return product(jnp.concatenate(columns, 0), back, 0)


def element_tiles(tile_ref, forces, source_ref, step):
    count = forces.shape[0] // FIELDS
    tile_ref[...] = jnp.zeros_like(tile_ref)
    for r in range(FIELDS):
        tile_ref[pl.ds(r, count, stride=8), :] = forces[r * count : (r + 1) * count]
    for j in range(3):
        row = count * 8 + 3 + j
        tile_ref[row : row + 1, :] = source_ref[j, step : step + 1, :]
    return [tile_ref[8 * t : 8 * t + 8, :] for t in range(count + 1)]


def block(c):
    return slice(c * WIDE, (c + 1) * WIDE)


def even_partition():
    return lax.rem(lax.axis_index("mesh"), 2) == 0


def halves_in_order(value, even):
    first, second = value[:HALF], value[HALF:]
    return [jnp.where(even, second, first), jnp.where(even, first, second)]


def first_kernel(*refs):
    inputs, refs = refs[:14], refs[14:]
    wave, local, scale, index, to_inner, to_outer, totals = refs[:7]
    source, ahead, back = kept = refs[7:10]
    arrived = refs[10:21]
    before, tiles, sems = refs[21:]
    copies = [
        pltpu.make_async_copy(value, target, sems.at[i])
        for i, (value, target) in enumerate(zip(inputs, arrived + kept))
    ]
    for i in (2, 0, 1, 6, 7, 12, 13, 4, 5, 3, 11, 8, 9, 10):
        copies[i].start()
    forward, adjoint, connectivity, receivers, lower, upper, bulk_modulus, shear_modulus = arrived[:8]
    forward_prev, adjoint_prev, step_scale = arrived[8:]
    sent = (to_inner, to_outer)
    for ref in (wave, before, scale):
        ref[...] = jnp.zeros_like(ref)
    for ref in sent:
        ref[SENT_KAPPA:SENT_SLOTS, :] = jnp.zeros((2 * HALF, LANES), F32)
        ref[SENT_SOURCE:, :] = jnp.zeros((8, LANES), F32)
    index[0:FACE_ROW, :] = jnp.zeros((FACE_ROW, LANES), jnp.int32)
    index[FACE_ROW:, :] = jnp.full((8, LANES), -1, jnp.int32)
    for copy in copies[:8]:
        copy.wait()
    for j in range(3):
        wave[j : j + 1, 0:POINTS] = forward[j]
        wave[3 + j : 4 + j, 0:POINTS] = adjoint[j]
    even = even_partition()
    for face, (part, kappa, shear_mod) in enumerate(
        zip(*(halves_in_order(ref[...], even) for ref in (connectivity, bulk_modulus, shear_modulus)))
    ):
        index[face * HALF : (face + 1) * HALF, 0:CUBE] = part
        sent[face][SENT_KAPPA : SENT_KAPPA + HALF, 0:CUBE] = kappa
        sent[face][SENT_SHEAR : SENT_SHEAR + HALF, 0:CUBE] = shear_mod
    index[RECEIVER_ROW : RECEIVER_ROW + 1, :] = receivers[...]
    index[PARITY_ROW : PARITY_ROW + 1, :] = jnp.where(even, jnp.ones((1, LANES), jnp.int32), 0)
    faces = (jnp.where(even, upper[...], lower[...]), jnp.where(even, lower[...], upper[...]))
    for t in range(3):
        size = min(LANES, FACE - t * LANES)
        for face in range(2):
            at = FACE_ROW + 3 * face + t
            index[at : at + 1, 0:size] = faces[face][:, t * LANES : t * LANES + size]
    kappa = jnp.concatenate([ref[SENT_KAPPA : SENT_KAPPA + HALF, :] for ref in sent], 0)
    shear_mod = jnp.concatenate([ref[SENT_SHEAR : SENT_SHEAR + HALF, :] for ref in sent], 0)
    fields = gather_elements(wave, index, FIELDS)
    for copy in copies[8:]:
        copy.wait()
    for j in range(3):
        before[j : j + 1, 0:POINTS] = forward_prev[j]
        before[3 + j : 4 + j, 0:POINTS] = adjoint_prev[j]
    scale[0:1, 0:POINTS] = step_scale[...].reshape(1, POINTS)
    strained = strains(fields, ahead[...])
    bulk, shear = kernel_terms(strained, kappa, shear_mod)
    totals[0:ELEMS, :] = bulk
    totals[ELEMS : 2 * ELEMS, :] = shear
    forces = element_forces(strained, kappa, shear_mod, back[...])
    row = lax.broadcasted_iota(jnp.int32, (8, LANES), 0)
    lane = lax.broadcasted_iota(jnp.int32, (8, LANES), 1)
    marks = [
        jnp.where(row == SLOT_ROW, lane + (face * OUTER + t * LANES + 1), 0).astype(F32)
        for face in range(2)
        for t in range(3)
    ]
    values = element_tiles(tiles, forces, source, 0) + marks
    rows = [index[t : t + 1, :] for t in range(RECEIVER_ROW + 1)]
    rows += [index[FACE_ROW + t : FACE_ROW + t + 1, :] for t in range(6)]
    forces = scatter(values, rows)
    wide_row = lax.broadcasted_iota(jnp.int32, (8, WIDE), 0)
    at_faces = []
    for c in range(COARSE):
        factor = jnp.broadcast_to(scale[0:1, block(c)], (8, WIDE))
        local[:, block(c)] = jnp.where(
            wide_row == SLOT_ROW,
            forces[c],
            2.0 * wave[:, block(c)] - before[:, block(c)] + factor * forces[c],
        )
        at_faces.append(jnp.where(wide_row == SCALE_ROW, factor, forces[c]))
    gather_faces(at_faces, index, sent)
    receiver = jnp.broadcast_to(index[RECEIVER_ROW : RECEIVER_ROW + 1, :], (8, LANES))
    held = jnp.zeros((8, LANES), F32)
    for c in range(FINE):
        mark = local[SLOT_ROW : SLOT_ROW + 1, c * LANES : (c + 1) * LANES]
        got = pick(jnp.broadcast_to(mark, (8, LANES)), receiver & 127)
        held = jnp.where(receiver >> 7 == c, got, held)
    held = held[0:1]
    for face in range(2):
        for j in range(3):
            sent[face][SENT_SOURCE + j : SENT_SOURCE + j + 1, :] = source[j, 1:2, :]
        own = held < OUTER if face == 0 else held > OUTER
        sent[face][SENT_SOURCE + 3 : SENT_SOURCE + 4, :] = jnp.where(own, held - face * OUTER, 0.0)
    for r, value in enumerate(gather_elements(local, index, FIELDS + 1)):
        start = SENT_SLOTS if r == SLOT_ROW else r * HALF
        for face in range(2):
            part = value[face * HALF : (face + 1) * HALF]
            if r == SLOT_ROW and face:
                part = jnp.maximum(part - OUTER, 0.0)
            sent[face][start : start + HALF, :] = part


def slot_picks(ref):
    slots = ref[SENT_SLOTS : SENT_SLOTS + HALF, :].astype(jnp.int32) - 1
    return (slots >> 7, slots & 127)


def scaled_forces(own, other):
    added = []
    for t in range(3):
        at = SENT_FACE + 8 * t
        added.append(own[at + SCALE_ROW : at + SCALE_ROW + 1, :] * other[at : at + 8, :])
    return added


def completed(own, added):
    fine, lane = slot_picks(own)
    fields = []
    for r in range(FIELDS):
        value = own[r * HALF : (r + 1) * HALF, :]
        for t in range(3):
            got = pick(jnp.broadcast_to(added[t][r : r + 1, :], (HALF, LANES)), lane)
            value = value + jnp.where(fine == t, got, 0.0)
        fields.append(value)
    return fields


def both(first, second, start):
    return jnp.concatenate([ref[start : start + HALF, :] for ref in (first, second)], 0)


def second_kernel(added_inner, from_outer, to_inner, to_outer, earlier, ahead, index, terms, now, sums):
    inner = completed(to_inner, [added_inner[8 * t : 8 * t + 8, :] for t in range(3)])
    outer = completed(to_outer, scaled_forces(to_outer, from_outer))
    fields = [jnp.concatenate(pair, 0) for pair in zip(inner, outer)]
    for r in range(FIELDS):
        now[r * ELEMS : (r + 1) * ELEMS, :] = fields[r]
    kappa = both(to_inner, to_outer, SENT_KAPPA)
    shear_mod = both(to_inner, to_outer, SENT_SHEAR)
    found = kernel_terms(strains(fields, ahead[...]), kappa, shear_mod)
    even = jnp.broadcast_to(index[PARITY_ROW : PARITY_ROW + 1, :], (HALF, LANES)) == 1
    for which in range(2):
        start = which * ELEMS
        total = earlier[start : start + ELEMS, :] + found[which]
        sums[start : start + ELEMS, :] = jnp.concatenate(halves_in_order(total, even), 0)
    for which in range(2):
        for e in range(2):
            start = which * ELEMS + e
            for place, event in enumerate(ORDER[::4]):
                terms[4 * place : 4 * place + 4, 2 * which + e, :] = sums[
                    pl.ds(start + 2 * event, 4, stride=2), :
                ]


def third_kernel(
    from_inner,
    from_outer,
    to_inner,
    to_outer,
    now,
    wave,
    local,
    scale,
    index,
    source,
    ahead,
    back,
    forward,
    adjoint,
    result,
    tiles,
):
    halo = [
        completed(own, scaled_forces(own, other))
        for own, other in ((from_inner, to_inner), (from_outer, to_outer))
    ]
    fields = [
        jnp.concatenate([now[r * ELEMS : (r + 1) * ELEMS, :], halo[0][r], halo[1][r]], 0)
        for r in range(FIELDS)
    ]
    moduli = [
        jnp.concatenate([both(to_inner, to_outer, start), both(from_inner, from_outer, start)], 0)
        for start in (SENT_KAPPA, SENT_SHEAR)
    ]
    forces = element_forces(strains(fields, ahead[...]), *moduli, back[...])
    values = element_tiles(tiles, forces, source, 1)
    rows = [index[t : t + 1, :] for t in range(ELEMS)]
    faces = []
    for face, ref in enumerate((from_inner, from_outer)):
        fine, lane = slot_picks(ref)
        heard = ref[SENT_SOURCE + 3 : SENT_SOURCE + 4, :].astype(jnp.int32) - 1
        heard = jnp.broadcast_to(heard, (8, LANES))
        points = jnp.full((HALF, LANES), -1, jnp.int32)
        receivers = jnp.full((8, LANES), -1, jnp.int32)
        for t in range(3):
            at = FACE_ROW + 3 * face + t
            row = index[at : at + 1, :]
            points = jnp.where(fine == t, pick(jnp.broadcast_to(row, (HALF, LANES)), lane), points)
            got = pick(jnp.broadcast_to(row, (8, LANES)), heard & 127)
            receivers = jnp.where(heard >> 7 == t, got, receivers)
            values.append(2.0 * ref[SENT_FACE + 8 * t : SENT_FACE + 8 * t + 8, :])
            faces.append(row)
        rows += [points[t : t + 1, :] for t in range(HALF)]
        source_tile = ref[SENT_SOURCE : SENT_SOURCE + 8, :]
        values.append(jnp.concatenate([jnp.zeros((3, LANES), F32), source_tile[0:3], source_tile[4:6]], 0))
        faces.append(receivers[0:1])
    rows += [index[RECEIVER_ROW : RECEIVER_ROW + 1, :]] + faces
    added = scatter(values, rows)
    for c in range(COARSE):
        result[:, block(c)] = (
            2.0 * local[:, block(c)] - wave[:, block(c)] + scale[0:1, block(c)] * added[c]
        )
    for j in range(3):
        forward[j] = result[j : j + 1, 0:POINTS]
        adjoint[j] = result[3 + j : 4 + j, 0:POINTS]


def call(kernel, outs, scratch, args, place=VMEM):
    return pl.pallas_call(
        kernel,
        out_shape=[jax.ShapeDtypeStruct(shape, dtype) for shape, dtype in outs],
        in_specs=[place] * len(args),
        out_specs=[VMEM] * len(outs),
        scratch_shapes=scratch,
        compiler_params=pltpu.CompilerParams(vmem_limit_bytes=24 * MIB),
    )(*args)


def swap_faces(to_inner, to_outer):
    count = lax.axis_size("mesh")
    inner = [(i, i ^ 1) for i in range(count)]
    outer = [(i, i + 1 if i % 2 else i - 1) for i in range(1, count - 1)]
    return (lax.ppermute(to_inner, "mesh", inner), lax.ppermute(to_outer, "mesh", outer))


def shards(
    forward_now,
    forward_prev,
    adjoint_now,
    adjoint_prev,
    connectivity,
    lower_face,
    upper_face,
    bulk_modulus,
    shear_modulus,
    step_scale,
    receiver_points,
    adjoint_source,
):
    def rows(field):
        return field.transpose(1, 0, 2)

    padded = ((8, PADDED), F32)
    sent = ((SENT, LANES), F32)
    pair = ((2 * ELEMS, LANES), F32)
    inputs = [
        rows(forward_now),
        rows(adjoint_now),
        connectivity.T,
        receiver_points.reshape(1, LANES),
        lower_face,
        upper_face,
        bulk_modulus.T,
        shear_modulus.T,
        rows(forward_prev),
        rows(adjoint_prev),
        step_scale,
        adjoint_source[0].transpose(1, 0, 2),
        *cube_tables(),
    ]
    inputs = [pltpu.with_memory_space_constraint(value, pltpu.HBM) for value in inputs]
    wave, local, scale, index, to_inner, to_outer, earlier, source, ahead, back = call(
        first_kernel,
        [padded, padded, ((1, PADDED), F32), ((48, LANES), jnp.int32), sent, sent, pair]
        + [(value.shape, value.dtype) for value in inputs[11:]],
        [pltpu.VMEM(value.shape, value.dtype) for value in inputs[:11]]
        + [pltpu.VMEM(*padded)]
        + [pltpu.VMEM(((ELEMS + 1) * 8, LANES), F32)]
        + [pltpu.SemaphoreType.DMA((len(inputs),))],
        inputs,
        pl.BlockSpec(memory_space=pl.ANY),
    )
    from_inner, from_outer = swap_faces(to_inner, to_outer)
    added_inner = jnp.concatenate(scaled_forces(to_inner, from_inner), 0)
    terms, now = call(
        second_kernel,
        [((EVENTS, 4, LANES), F32), ((FIELDS * ELEMS, LANES), F32)],
        [pltpu.VMEM(*pair)],
        [added_inner, from_outer, to_inner, to_outer, earlier, ahead, index],
    )
    terms = lax.all_to_all(terms, "event", 0, 0, axis_index_groups=[ORDER], tiled=True)
    forward, adjoint = call(
        third_kernel,
        [((3, 1, POINTS), F32), ((3, 1, POINTS), F32)],
        [pltpu.VMEM(*padded), pltpu.VMEM(((2 * ELEMS + 1) * 8, LANES), F32)],
        [from_inner, from_outer, to_inner, to_outer, now, wave, local, scale, index, source, ahead, back],
    )
    kernels = jnp.sum(terms, axis=0)[:, :CUBE].reshape(2, 2, CUBE)
    return (rows(forward), rows(adjoint), kernels.transpose(0, 2, 1))


def solution(mesh):
    placed = (
        P("event", None, "mesh"),
        P("event", None, "mesh"),
        P("event", None, "mesh"),
        P("event", None, "mesh"),
        P(None, "mesh"),
        P("mesh", None),
        P("mesh", None),
        P(None, "mesh"),
        P(None, "mesh"),
        P("mesh"),
        P("mesh"),
        P("event", None, None, "mesh"),
    )
    return jax.shard_map(
        shards,
        mesh=mesh,
        in_specs=placed,
        out_specs=(
            P("event", None, "mesh"),
            P("event", None, "mesh"),
            P(None, None, ("mesh", "event")),
        ),
        check_vma=False,
    )
```

```python
import functools
import math

import jax
import jax.numpy as jnp
import numpy as np
from jax import lax
from jax.experimental import pallas as pl
from jax.experimental.pallas import tpu as pltpu
from jax.sharding import PartitionSpec as P

F32 = jnp.float32
BF16 = jnp.bfloat16
EVENTS = 16
FIELDS = 6
ELEMS = 32
CUBE = 125
POINTS = 2601
FACE = 289
LANES = 128
WIDE = 256
FINE = 21
COARSE = 11
PADDED = COARSE * WIDE
HALF = 16
RECEIVER_ROW = 32
FACE_ROW = 40
PARITY_ROW = 46
SLOT_ROW = 6
SCALE_ROW = 7
OUTER = 512
ORDER = [10, 8, 9, 11, 12, 13, 14, 15, 0, 1, 2, 3, 4, 5, 6, 7]
SENT_KAPPA = FIELDS * HALF
SENT_SHEAR = SENT_KAPPA + HALF
SENT_SLOTS = SENT_SHEAR + HALF
SENT_FACE = SENT_SLOTS + HALF
SENT_SOURCE = SENT_FACE + 24
SENT = SENT_SOURCE + 8
CHUNK = 8
KERNEL_WEIGHT = 0.02

VMEM = pl.BlockSpec(memory_space=pltpu.VMEM)
MIB = 1024 * 1024


def derivative_table():
    root = math.sqrt(3.0 / 7.0)
    points = [-1.0, -root, 0.0, root, 1.0]
    legendre = [(35.0 * x**4 - 30.0 * x**2 + 3.0) / 8.0 for x in points]
    table = np.zeros((5, 5))
    for row in range(5):
        for column in range(5):
            if row != column:
                table[row, column] = (
                    legendre[row] / legendre[column] / (points[row] - points[column])
                )
    table[0, 0] = -2.5
    table[4, 4] = 2.5
    return table


def cube_tables():
    deriv = derivative_table().astype(np.float32).astype(np.float64)
    line = np.array([0.1, 49.0 / 90.0, 32.0 / 45.0, 49.0 / 90.0, 0.1])
    cube = (line[:, None, None] * line[None, :, None] * line[None, None, :]).reshape(CUBE)
    cube = cube.astype(np.float32).astype(np.float64)
    along = [
        np.kron(np.eye(25), deriv),
        np.kron(np.eye(5), np.kron(deriv, np.eye(5))),
        np.kron(deriv, np.eye(25)),
    ]
    ahead = np.zeros((3 * LANES, LANES))
    back = np.zeros((3 * LANES, LANES))
    for i in range(3):
        ahead[i * LANES : i * LANES + CUBE, :CUBE] = along[i]
        back[i * LANES : i * LANES + CUBE, :CUBE] = -cube[:, None] * along[i]
    return (jnp.asarray(ahead, F32), jnp.asarray(back, F32))


def split(value):
    high = value.astype(BF16)
    return (high, (value - high.astype(F32)).astype(BF16))


def product(value, table, side):
    high, low = split(value)
    table_high, table_low = split(table)

    def dot(a, b):
        return lax.dot_general(a, b, (((1,), (side,)), ((), ())), preferred_element_type=F32)

    return dot(high, table_high) + (dot(low, table_high) + dot(high, table_low))


def pick(row, lanes):
    return jnp.take_along_axis(row, lanes, axis=1, mode="promise_in_bounds")


def gather_elements(wave_ref, index_ref, count):
    groups = []
    for t in range(0, ELEMS, 8):
        index = index_ref[t : t + 8, :]
        fine = index >> 7
        lane = index & 127
        found = [jnp.zeros((8, LANES), F32) for _ in range(count)]
        for c in range(FINE):
            hit = fine == c
            for r in range(count):
                row = wave_ref[r : r + 1, c * LANES : (c + 1) * LANES]
                found[r] = jnp.where(hit, pick(jnp.broadcast_to(row, (8, LANES)), lane), found[r])
        groups.append(found)
    return [jnp.concatenate(parts, 0) for parts in zip(*groups)]


def gather_faces(blocks, index_ref, targets):
    for face in range(2):
        for tile in range(3):
            at = FACE_ROW + 3 * face + tile
            index = jnp.broadcast_to(index_ref[at : at + 1, :], (8, LANES))
            fine = index >> 7
            lane = index & 127
            found = jnp.zeros((8, LANES), F32)
            for c in range(FINE):
                part = slice((c % 2) * LANES, (c % 2 + 1) * LANES)
                found = jnp.where(fine == c, pick(blocks[c // 2][:, part], lane), found)
            targets[face][SENT_FACE + 8 * tile : SENT_FACE + 8 * tile + 8, :] = found


def scatter(tiles, rows, blocks=COARSE, width=WIDE):
    shift = width.bit_length() - 1
    step = lax.broadcasted_iota(jnp.int32, (16, LANES), 0)
    total = None
    for start in range(0, len(tiles), CHUNK):
        left = []
        right = []
        for tile, row in zip(tiles[start : start + CHUNK], rows[start : start + CHUNK]):
            index = jnp.broadcast_to(row, (16, LANES))
            coarse = (index >> shift).astype(F32).astype(BF16)
            offset = ((index & (width - 1)) - step).astype(F32).astype(BF16)
            high = tile.astype(BF16).astype(F32)
            pair = jnp.concatenate([high, tile - high], 0).astype(BF16)
            none = jnp.zeros_like(pair)
            one = jnp.ones_like(pair)
            left.append(jnp.concatenate([jnp.where(coarse == c, pair, none) for c in range(blocks)], 0))
            right.append(jnp.concatenate([jnp.where(offset == c * 16, one, none) for c in range(width // 16)], 0))
        part = lax.dot_general(
            jnp.concatenate(left, 1),
            jnp.concatenate(right, 1),
            (((1,), (1,)), ((), ())),
            preferred_element_type=F32,
        )
        total = part if total is None else total + part
    return [total[c * 16 : c * 16 + 8] + total[c * 16 + 8 : c * 16 + 16] for c in range(blocks)]


def strains(fields, ahead):
    count = fields[0].shape[0]
    grads = product(jnp.concatenate(fields, 0), ahead, 1)

    def grad(f, i, j):
        r = (3 * f + j) * count
        return grads[r : r + count, i * LANES : (i + 1) * LANES]

    result = []
    for f in range(2):
        normal = [grad(f, i, i) for i in range(3)]
        dilation = normal[0] + normal[1] + normal[2]
        deviator = [n - dilation * (1.0 / 3.0) for n in normal]
        shear = {
            (i, j): 0.5 * (grad(f, i, j) + grad(f, j, i)) for i, j in ((0, 1), (0, 2), (1, 2))
        }
        result.append((dilation, deviator, shear))
    return result


def kernel_terms(strained, kappa, shear_mod):
    (dilation0, normal0, shear0), (dilation1, normal1, shear1) = strained
    bulk = -KERNEL_WEIGHT * kappa * dilation0 * dilation1
    inner = normal0[0] * normal1[0] + normal0[1] * normal1[1] + normal0[2] * normal1[2]
    cross = sum(shear0[key] * shear1[key] for key in shear0)
    return (bulk, -2.0 * KERNEL_WEIGHT * shear_mod * (inner + 2.0 * cross))


def element_forces(strained, kappa, shear_mod, back):
    twice = 2.0 * shear_mod
    columns = []
    for dilation, deviator, shear in strained:
        pressure = kappa * dilation
        for j in range(3):
            stress = [
                pressure + twice * deviator[j] if i == j else twice * shear[min(i, j), max(i, j)]
                for i in range(3)
            ]
            columns.append(jnp.concatenate(stress, 1))
    return product(jnp.concatenate(columns, 0), back, 0)


def element_tiles(tile_ref, forces, source_ref, step):
    count = forces.shape[0] // FIELDS
    tile_ref[...] = jnp.zeros_like(tile_ref)
    for r in range(FIELDS):
        tile_ref[pl.ds(r, count, stride=8), :] = forces[r * count : (r + 1) * count]
    for j in range(3):
        row = count * 8 + 3 + j
        tile_ref[row : row + 1, :] = source_ref[j, step : step + 1, :]
    return [tile_ref[8 * t : 8 * t + 8, :] for t in range(count + 1)]


def block(c):
    return slice(c * WIDE, (c + 1) * WIDE)


def even_partition():
    return lax.rem(lax.axis_index("mesh"), 2) == 0


def halves_in_order(value, even):
    first, second = value[:HALF], value[HALF:]
    return [jnp.where(even, second, first), jnp.where(even, first, second)]


def first_kernel(*refs):
    inputs, refs = refs[:14], refs[14:]
    wave, local, scale, index, to_inner, to_outer, totals = refs[:7]
    source, ahead, back = kept = refs[7:10]
    arrived = refs[10:21]
    before, tiles, sems = refs[21:]
    copies = [
        pltpu.make_async_copy(value, target, sems.at[i])
        for i, (value, target) in enumerate(zip(inputs, arrived + kept))
    ]
    for i in (2, 0, 1, 6, 7, 12, 13, 4, 5, 3, 11, 8, 9, 10):
        copies[i].start()
    forward, adjoint, connectivity, receivers, lower, upper, bulk_modulus, shear_modulus = arrived[:8]
    forward_prev, adjoint_prev, step_scale = arrived[8:]
    sent = (to_inner, to_outer)
    for ref in (wave, before, scale):
        ref[...] = jnp.zeros_like(ref)
    for ref in sent:
        ref[SENT_KAPPA:SENT_SLOTS, :] = jnp.zeros((2 * HALF, LANES), F32)
        ref[SENT_SOURCE:, :] = jnp.zeros((8, LANES), F32)
    index[0:FACE_ROW, :] = jnp.zeros((FACE_ROW, LANES), jnp.int32)
    index[FACE_ROW:, :] = jnp.full((8, LANES), -1, jnp.int32)
    for copy in copies[:8]:
        copy.wait()
    for j in range(3):
        wave[j : j + 1, 0:POINTS] = forward[j]
        wave[3 + j : 4 + j, 0:POINTS] = adjoint[j]
    even = even_partition()
    for face, (part, kappa, shear_mod) in enumerate(
        zip(*(halves_in_order(ref[...], even) for ref in (connectivity, bulk_modulus, shear_modulus)))
    ):
        index[face * HALF : (face + 1) * HALF, 0:CUBE] = part
        sent[face][SENT_KAPPA : SENT_KAPPA + HALF, 0:CUBE] = kappa
        sent[face][SENT_SHEAR : SENT_SHEAR + HALF, 0:CUBE] = shear_mod
    index[RECEIVER_ROW : RECEIVER_ROW + 1, :] = receivers[...]
    index[PARITY_ROW : PARITY_ROW + 1, :] = jnp.where(even, jnp.ones((1, LANES), jnp.int32), 0)
    faces = (jnp.where(even, upper[...], lower[...]), jnp.where(even, lower[...], upper[...]))
    for t in range(3):
        size = min(LANES, FACE - t * LANES)
        for face in range(2):
            at = FACE_ROW + 3 * face + t
            index[at : at + 1, 0:size] = faces[face][:, t * LANES : t * LANES + size]
    kappa = jnp.concatenate([ref[SENT_KAPPA : SENT_KAPPA + HALF, :] for ref in sent], 0)
    shear_mod = jnp.concatenate([ref[SENT_SHEAR : SENT_SHEAR + HALF, :] for ref in sent], 0)
    fields = gather_elements(wave, index, FIELDS)
    for copy in copies[8:]:
        copy.wait()
    for j in range(3):
        before[j : j + 1, 0:POINTS] = forward_prev[j]
        before[3 + j : 4 + j, 0:POINTS] = adjoint_prev[j]
    scale[0:1, 0:POINTS] = step_scale[...].reshape(1, POINTS)
    strained = strains(fields, ahead[...])
    bulk, shear = kernel_terms(strained, kappa, shear_mod)
    totals[0:ELEMS, :] = bulk
    totals[ELEMS : 2 * ELEMS, :] = shear
    forces = element_forces(strained, kappa, shear_mod, back[...])
    row = lax.broadcasted_iota(jnp.int32, (8, LANES), 0)
    lane = lax.broadcasted_iota(jnp.int32, (8, LANES), 1)
    marks = [
        jnp.where(row == SLOT_ROW, lane + (face * OUTER + t * LANES + 1), 0).astype(F32)
        for face in range(2)
        for t in range(3)
    ]
    values = element_tiles(tiles, forces, source, 0) + marks
    rows = [index[t : t + 1, :] for t in range(RECEIVER_ROW + 1)]
    rows += [index[FACE_ROW + t : FACE_ROW + t + 1, :] for t in range(6)]
    forces = scatter(values, rows)
    wide_row = lax.broadcasted_iota(jnp.int32, (8, WIDE), 0)
    at_faces = []
    for c in range(COARSE):
        factor = jnp.broadcast_to(scale[0:1, block(c)], (8, WIDE))
        local[:, block(c)] = jnp.where(
            wide_row == SLOT_ROW,
            forces[c],
            2.0 * wave[:, block(c)] - before[:, block(c)] + factor * forces[c],
        )
        at_faces.append(jnp.where(wide_row == SCALE_ROW, factor, forces[c]))
    gather_faces(at_faces, index, sent)
    receiver = jnp.broadcast_to(index[RECEIVER_ROW : RECEIVER_ROW + 1, :], (8, LANES))
    held = jnp.zeros((8, LANES), F32)
    for c in range(FINE):
        mark = local[SLOT_ROW : SLOT_ROW + 1, c * LANES : (c + 1) * LANES]
        got = pick(jnp.broadcast_to(mark, (8, LANES)), receiver & 127)
        held = jnp.where(receiver >> 7 == c, got, held)
    held = held[0:1]
    for face in range(2):
        for j in range(3):
            sent[face][SENT_SOURCE + j : SENT_SOURCE + j + 1, :] = source[j, 1:2, :]
        own = held < OUTER if face == 0 else held > OUTER
        sent[face][SENT_SOURCE + 3 : SENT_SOURCE + 4, :] = jnp.where(own, held - face * OUTER, 0.0)
    for r, value in enumerate(gather_elements(local, index, FIELDS + 1)):
        start = SENT_SLOTS if r == SLOT_ROW else r * HALF
        for face in range(2):
            part = value[face * HALF : (face + 1) * HALF]
            if r == SLOT_ROW and face:
                part = jnp.maximum(part - OUTER, 0.0)
            sent[face][start : start + HALF, :] = part


def slot_picks(ref):
    slots = ref[SENT_SLOTS : SENT_SLOTS + HALF, :].astype(jnp.int32) - 1
    return (slots >> 7, slots & 127)


def scaled_forces(own, other):
    added = []
    for t in range(3):
        at = SENT_FACE + 8 * t
        added.append(own[at + SCALE_ROW : at + SCALE_ROW + 1, :] * other[at : at + 8, :])
    return added


def completed(own, added):
    fine, lane = slot_picks(own)
    fields = []
    for r in range(FIELDS):
        value = own[r * HALF : (r + 1) * HALF, :]
        for t in range(3):
            got = pick(jnp.broadcast_to(added[t][r : r + 1, :], (HALF, LANES)), lane)
            value = value + jnp.where(fine == t, got, 0.0)
        fields.append(value)
    return fields


def both(first, second, start):
    return jnp.concatenate([ref[start : start + HALF, :] for ref in (first, second)], 0)


def second_kernel(added_inner, from_outer, to_inner, to_outer, earlier, ahead, index, terms, now, sums):
    inner = completed(to_inner, [added_inner[8 * t : 8 * t + 8, :] for t in range(3)])
    outer = completed(to_outer, scaled_forces(to_outer, from_outer))
    fields = [jnp.concatenate(pair, 0) for pair in zip(inner, outer)]
    for r in range(FIELDS):
        now[r * ELEMS : (r + 1) * ELEMS, :] = fields[r]
    kappa = both(to_inner, to_outer, SENT_KAPPA)
    shear_mod = both(to_inner, to_outer, SENT_SHEAR)
    found = kernel_terms(strains(fields, ahead[...]), kappa, shear_mod)
    even = jnp.broadcast_to(index[PARITY_ROW : PARITY_ROW + 1, :], (HALF, LANES)) == 1
    for which in range(2):
        start = which * ELEMS
        total = earlier[start : start + ELEMS, :] + found[which]
        sums[start : start + ELEMS, :] = jnp.concatenate(halves_in_order(total, even), 0)
    for which in range(2):
        for e in range(2):
            start = which * ELEMS + e
            for place, event in enumerate(ORDER):
                row = start + 2 * event
                terms[place, 2 * which + e : 2 * which + e + 1, :] = sums[row : row + 1, :]


def third_kernel(
    from_inner,
    from_outer,
    to_inner,
    to_outer,
    now,
    wave,
    local,
    scale,
    index,
    source,
    ahead,
    back,
    forward,
    adjoint,
    result,
    tiles,
):
    halo = [
        completed(own, scaled_forces(own, other))
        for own, other in ((from_inner, to_inner), (from_outer, to_outer))
    ]
    fields = [
        jnp.concatenate([now[r * ELEMS : (r + 1) * ELEMS, :], halo[0][r], halo[1][r]], 0)
        for r in range(FIELDS)
    ]
    moduli = [
        jnp.concatenate([both(to_inner, to_outer, start), both(from_inner, from_outer, start)], 0)
        for start in (SENT_KAPPA, SENT_SHEAR)
    ]
    forces = element_forces(strains(fields, ahead[...]), *moduli, back[...])
    everything = element_tiles(tiles, forces, source, 1)
    values = everything[:ELEMS] + everything[2 * ELEMS :]
    rows = [index[t : t + 1, :] for t in range(RECEIVER_ROW + 1)]
    for face, ref in enumerate((from_inner, from_outer)):
        start = ELEMS + face * HALF
        slots = ref[SENT_SLOTS : SENT_SLOTS + HALF, :].astype(jnp.int32) - 1
        held = scatter(everything[start : start + HALF], [slots[t : t + 1, :] for t in range(HALF)], 3, LANES)
        heard = ref[SENT_SOURCE + 3 : SENT_SOURCE + 4, :].astype(jnp.int32) - 1
        heard = jnp.broadcast_to(heard, (8, LANES))
        receivers = jnp.full((8, LANES), -1, jnp.int32)
        for t in range(3):
            at = FACE_ROW + 3 * face + t
            row = index[at : at + 1, :]
            got = pick(jnp.broadcast_to(row, (8, LANES)), heard & 127)
            receivers = jnp.where(heard >> 7 == t, got, receivers)
            values.append(held[t] + 2.0 * ref[SENT_FACE + 8 * t : SENT_FACE + 8 * t + 8, :])
            rows.append(row)
        source_tile = ref[SENT_SOURCE : SENT_SOURCE + 8, :]
        values.append(jnp.concatenate([jnp.zeros((3, LANES), F32), source_tile[0:3], source_tile[4:6]], 0))
        rows.append(receivers[0:1])
    added = scatter(values, rows)
    for c in range(COARSE):
        result[:, block(c)] = (
            2.0 * local[:, block(c)] - wave[:, block(c)] + scale[0:1, block(c)] * added[c]
        )
    for j in range(3):
        forward[j] = result[j : j + 1, 0:POINTS]
        adjoint[j] = result[3 + j : 4 + j, 0:POINTS]


def call(kernel, outs, scratch, args, place=VMEM):
    return pl.pallas_call(
        kernel,
        out_shape=[jax.ShapeDtypeStruct(shape, dtype) for shape, dtype in outs],
        in_specs=[place] * len(args),
        out_specs=[VMEM] * len(outs),
        scratch_shapes=scratch,
        compiler_params=pltpu.CompilerParams(vmem_limit_bytes=24 * MIB),
    )(*args)


def swap_faces(to_inner, to_outer):
    count = lax.axis_size("mesh")
    inner = [(i, i ^ 1) for i in range(count)]
    outer = [(i, i + 1 if i % 2 else i - 1) for i in range(1, count - 1)]
    return (lax.ppermute(to_inner, "mesh", inner), lax.ppermute(to_outer, "mesh", outer))


def shards(
    forward_now,
    forward_prev,
    adjoint_now,
    adjoint_prev,
    connectivity,
    lower_face,
    upper_face,
    bulk_modulus,
    shear_modulus,
    step_scale,
    receiver_points,
    adjoint_source,
):
    def rows(field):
        return field.transpose(1, 0, 2)

    padded = ((8, PADDED), F32)
    sent = ((SENT, LANES), F32)
    pair = ((2 * ELEMS, LANES), F32)
    inputs = [
        rows(forward_now),
        rows(adjoint_now),
        connectivity.T,
        receiver_points.reshape(1, LANES),
        lower_face,
        upper_face,
        bulk_modulus.T,
        shear_modulus.T,
        rows(forward_prev),
        rows(adjoint_prev),
        step_scale,
        adjoint_source[0].transpose(1, 0, 2),
        *cube_tables(),
    ]
    inputs = [pltpu.with_memory_space_constraint(value, pltpu.HBM) for value in inputs]
    wave, local, scale, index, to_inner, to_outer, earlier, source, ahead, back = call(
        first_kernel,
        [padded, padded, ((1, PADDED), F32), ((48, LANES), jnp.int32), sent, sent, pair]
        + [(value.shape, value.dtype) for value in inputs[11:]],
        [pltpu.VMEM(value.shape, value.dtype) for value in inputs[:11]]
        + [pltpu.VMEM(*padded)]
        + [pltpu.VMEM(((ELEMS + 1) * 8, LANES), F32)]
        + [pltpu.SemaphoreType.DMA((len(inputs),))],
        inputs,
        pl.BlockSpec(memory_space=pl.ANY),
    )
    from_inner, from_outer = swap_faces(to_inner, to_outer)
    added_inner = jnp.concatenate(scaled_forces(to_inner, from_inner), 0)
    terms, now = call(
        second_kernel,
        [((EVENTS, 4, LANES), F32), ((FIELDS * ELEMS, LANES), F32)],
        [pltpu.VMEM(*pair)],
        [added_inner, from_outer, to_inner, to_outer, earlier, ahead, index],
    )
    terms = lax.all_to_all(terms, "event", 0, 0, axis_index_groups=[ORDER], tiled=True)
    forward, adjoint = call(
        third_kernel,
        [((3, 1, POINTS), F32), ((3, 1, POINTS), F32)],
        [pltpu.VMEM(*padded), pltpu.VMEM(((2 * ELEMS + 1) * 8, LANES), F32)],
        [from_inner, from_outer, to_inner, to_outer, now, wave, local, scale, index, source, ahead, back],
    )
    kernels = jnp.sum(terms, axis=0)[:, :CUBE].reshape(2, 2, CUBE)
    return (rows(forward), rows(adjoint), kernels.transpose(0, 2, 1))


def solution(mesh):
    placed = (
        P("event", None, "mesh"),
        P("event", None, "mesh"),
        P("event", None, "mesh"),
        P("event", None, "mesh"),
        P(None, "mesh"),
        P("mesh", None),
        P("mesh", None),
        P(None, "mesh"),
        P(None, "mesh"),
        P("mesh"),
        P("mesh"),
        P("event", None, None, "mesh"),
    )
    return jax.shard_map(
        shards,
        mesh=mesh,
        in_specs=placed,
        out_specs=(
            P("event", None, "mesh"),
            P("event", None, "mesh"),
            P(None, None, ("mesh", "event")),
        ),
        check_vma=False,
    )
```
